256 devices in a mesh: rows: 32 (over x, z_lo, core), cols: 8 (over z_hi, y).
Axes of the slice: x: 4, y: 4, z: 8 (z_hi: 2, z_lo: 4; z = z_hi * 4 + z_lo), core: 2. Of those that a mesh axis runs over, the one named last changes fastest.
Arguments:
- row_factor: bfloat16 [65536, 512], P(('rows', 'cols')), may hold values from -1.1953125 to 1.1953125
- col_factor: bfloat16 [262144, 512], P(('rows', 'cols')), may hold values from -1.1953125 to 1.1953125
- tiles: bfloat16 [2, 32, 8, 16, 256, 256], P(None, 'rows', 'cols'), may hold values from -6 to 6
- tile_rows: int32 [2, 32, 8, 16], P(None, 'rows', 'cols'), may hold values from 0 to 7, as said below
- tile_cols: int32 [2, 32, 8, 16], P(None, 'rows', 'cols'), may hold values from 0 to 3, as said below
- tile_counts: int32 [2, 32, 8], P(None, 'rows', 'cols'), may hold values from 2 to 16, as said below
- matching: int32 [2, 32], replicated, may hold values from 0 to 31, as said below
- row_noise: bfloat16 [2, 65536, 512], P(None, ('rows', 'cols')), may hold values from -6 to 6
- col_noise: bfloat16 [2, 262144, 512], P(None, ('rows', 'cols')), may hold values from -6 to 6
- step_sizes: float32 [2], replicated, may hold values from 0.01 to 0.04
Outputs:
- row_sample: bfloat16 [65536, 512], P(('rows', 'cols'))
- col_sample: bfloat16 [262144, 512], P(('rows', 'cols'))
The draws below stay inside these ranges and needn't reach their ends.
Inputs may be any that keep to these rules, and one draw needn't show every extreme that they name: In each stratum, row block and panel, the 16 slots name distinct tile positions (tile_rows, tile_cols) among 8 x 4. `tile_cols`: see tile_rows. `tile_counts`: in each stratum some row block and panel have exactly 16 observed tiles; slots from the count on hold tiles that are not observed. matching[s, b] is b bitwise exclusive or matching[s, 0]; matching[1, b] is matching[0, b] bitwise exclusive or (31).
All inputs are finite; a program needn't handle non-finite values.
Results may differ from the reference program's by a relative error of at most 0.02.
Values may be sent and summed in bfloat16 or wider, within the bound.
No kernel may reach another device: no remote copies, remote signals or barrier semaphores. Data moves between devices by JAX's collectives and lax.ppermute only.
A program may use at most 64 MiB of HBM per device.

```python
import math
import jax
import jax.numpy as jnp
from jax import lax

K = 512
TILE = 256
RT = 8
CT = 4
STRATA = 2
BLOCKS = 32
PANELS = 8
TMAX = 16
ROWS_ALL = 65536
COLS_ALL = 262144


def position_table(key):
    positions_all = RT * CT
    scores = jax.random.randint(key, (STRATA, BLOCKS, PANELS, positions_all), 0, 1 << 20) * positions_all + jnp.arange(positions_all, dtype=jnp.int32)
    ordering = jnp.argsort(scores, axis=-1)
    return ordering[..., :TMAX].astype(jnp.int32)


def draw_tile_rows(key, part):
    return (position_table(key) // CT).astype(jnp.int32)


def draw_tile_cols(key, part):
    return (position_table(key) % CT).astype(jnp.int32)


def draw_tile_counts(key, part):
    key = jax.random.fold_in(key, 7)
    first_key, second_key, third_key = jax.random.split(key, 3)
    light_load = jax.random.randint(first_key, (STRATA, BLOCKS * PANELS), 2, TMAX // 3 + 3)
    heavy_load = jax.random.randint(second_key, (STRATA, BLOCKS * PANELS), 0, 8) == 0
    forced_index = jax.random.randint(third_key, (STRATA, 1), 0, BLOCKS * PANELS)
    forced = jnp.arange(BLOCKS * PANELS, dtype=jnp.int32)[None, :] == forced_index
    counts_all = jnp.where(heavy_load | forced, TMAX, light_load)
    return counts_all.reshape(STRATA, BLOCKS, PANELS).astype(jnp.int32)


def draw_matching(key, part):
    key = jax.random.fold_in(key, 11)
    first_mask = jax.random.randint(key, (), 0, BLOCKS).astype(jnp.int32)
    block_ids = jnp.arange(BLOCKS, dtype=jnp.int32)
    second_mask = jnp.bitwise_xor(first_mask, BLOCKS - 1)
    return jnp.stack([jnp.bitwise_xor(block_ids, first_mask), jnp.bitwise_xor(block_ids, second_mask)]).astype(jnp.int32)


def shard_levels(rng, extent, cuts, low, high):
    gain = 1.0
    for dim, parts in cuts:
        heights = jax.random.uniform(jax.random.fold_in(jax.random.fold_in(rng, 6), dim), (parts,), jnp.float32, low / len(cuts), high / len(cuts))
        gain = gain * jnp.repeat(jnp.exp(heights), extent[dim] // parts).reshape((-1,) + (1,) * (len(extent) - 1 - dim))
    return gain


def centred(stream_key, shape, width, bound, cuts=(), held_as=jnp.bfloat16):
    values = width * jax.random.normal(stream_key, shape, jnp.float32)
    if cuts:
        values = values * shard_levels(stream_key, shape, cuts, -0.22, 0.18)
    return jnp.clip(values, -bound, bound).astype(held_as)


def setup_inputs(seed: int = 0) -> dict:
    streams_of = jax.random.split(jax.random.key(seed), 11)
    return {
        "row_factor": centred(streams_of[0], (ROWS_ALL, K), 0.2, 1.1953125, ((0, 256),)),
        "col_factor": centred(streams_of[1], (COLS_ALL, K), 0.2, 1.1953125, ((0, 256),)),
        "tiles": centred(streams_of[2], (STRATA, BLOCKS, PANELS, TMAX, TILE, TILE), 1.0, 6.0, ((1, 32), (2, 8))),
        "tile_rows": draw_tile_rows(jax.random.fold_in(streams_of[10], 71), 0),
        "tile_cols": draw_tile_cols(jax.random.fold_in(streams_of[10], 71), 0),
        "tile_counts": draw_tile_counts(jax.random.fold_in(streams_of[10], 71), 0),
        "matching": draw_matching(jax.random.fold_in(streams_of[10], 71), 0),
        "row_noise": centred(streams_of[7], (STRATA, ROWS_ALL, K), 1.0, 6.0, ((1, 256),)),
        "col_noise": centred(streams_of[8], (STRATA, COLS_ALL, K), 1.0, 6.0, ((1, 256),)),
        "step_sizes": jnp.clip(jnp.exp(jax.random.uniform(streams_of[9], (STRATA,), jnp.float32, math.log(0.01), math.log(0.04))), 0.01, 0.04),
    }


prior_precision = 1.0

def langevin(current, gradient, gaussian, step_size):
    current_wide = current.astype(jnp.float32)
    moved = current_wide + 0.5 * step_size * (gradient - prior_precision * current_wide) + jnp.sqrt(step_size) * gaussian.astype(jnp.float32)
    return moved.astype(jnp.bfloat16)

def reference(row_factor, col_factor, tiles, tile_rows, tile_cols, tile_counts, matching, row_noise, col_noise, step_sizes):
    rows_now = row_factor
    cols_now = col_factor
    for stratum in range(STRATA):
        step_size = step_sizes[stratum]
        u_blocks = rows_now.reshape(BLOCKS, RT, TILE, K)
        v_blocks = cols_now.reshape(BLOCKS, PANELS, CT, TILE, K)
        matched = v_blocks[matching[stratum]]

        def one_block(block_items):
            u_block, v_block, data_tiles, row_pick, col_pick, tile_count, row_gauss, col_gauss = block_items
            u_sel = u_block[row_pick]
            v_sel = jnp.take_along_axis(v_block, col_pick[:, :, None, None], axis=1)
            predicted = jnp.einsum('ptak,ptbk->ptab', u_sel.astype(jnp.float32), v_sel.astype(jnp.float32))
            observed = jnp.arange(TMAX, dtype=jnp.int32)[None, :] < tile_count[:, None]
            residual = jnp.where(observed[:, :, None, None], data_tiles.astype(jnp.float32) - predicted, 0.0).astype(jnp.bfloat16)
            residual_wide = residual.astype(jnp.float32)
            row_terms = jnp.einsum('ptab,ptbk->ptak', residual_wide, v_sel.astype(jnp.float32))
            col_terms = jnp.einsum('ptab,ptak->ptbk', residual_wide, u_sel.astype(jnp.float32))
            row_hot = (row_pick[:, :, None] == jnp.arange(RT, dtype=jnp.int32)).astype(jnp.float32)
            col_hot = (col_pick[:, :, None] == jnp.arange(CT, dtype=jnp.int32)).astype(jnp.float32)
            row_partial = jnp.einsum('ptr,ptak->prak', row_hot, row_terms, precision=lax.Precision.HIGHEST).astype(jnp.bfloat16)
            row_grad = lax.optimization_barrier(jnp.sum(row_partial.astype(jnp.float32), axis=0))
            col_grad = jnp.einsum('ptc,ptbk->pcbk', col_hot, col_terms, precision=lax.Precision.HIGHEST)
            return (langevin(u_block, row_grad, row_gauss, step_size), langevin(v_block, col_grad, col_gauss, step_size))
        new_rows, new_cols = lax.map(one_block, (u_blocks, matched, tiles[stratum], tile_rows[stratum], tile_cols[stratum], tile_counts[stratum], row_noise[stratum].reshape(BLOCKS, RT, TILE, K), col_noise[stratum].reshape(BLOCKS, PANELS, CT, TILE, K)))
        rows_now = new_rows.reshape(BLOCKS * RT * TILE, K)
        cols_now = jnp.zeros_like(v_blocks).at[matching[stratum]].set(new_cols).reshape(BLOCKS * PANELS * CT * TILE, K)
    return (rows_now, cols_now)
```

```python
import functools

import jax
import jax.numpy as jnp
from jax import lax
from jax.experimental import pallas as pl
from jax.experimental.pallas import tpu as pltpu
from jax.sharding import PartitionSpec as P

TILE = 256
PEERS = 8
BLOCKS = 32

prior_precision = 1.0


def swap(value, axis, mask):
    return lax.ppermute(value, axis, [(i, i ^ mask) for i in range(lax.axis_size(axis))])


def langevin(current, gradient, gaussian, step_size):
    current_wide = current.astype(jnp.float32)
    return (
        current_wide
        + 0.5 * step_size * (gradient - prior_precision * current_wide)
        + jnp.sqrt(step_size) * gaussian.astype(jnp.float32)
    )


def gather_rows(shard):
    partner = swap(shard, "cols", 4)
    near = [swap(shard, "cols", k) for k in (1, 2, 3)]
    far = [swap(partner, "cols", k) for k in (1, 2, 3)]
    return [shard] + near + [partner] + far


def scatter_rows(parts):
    wide = lambda x: x.astype(jnp.float32)
    far = [swap(parts[4 + k], "cols", k) for k in (1, 2, 3)]
    far_sum = wide(parts[4]) + wide(far[0]) + wide(far[1]) + wide(far[2])
    partner = swap(far_sum.astype(jnp.bfloat16), "cols", 4)
    near = [swap(parts[k], "cols", k) for k in (1, 2, 3)]
    return wide(parts[0]) + wide(near[0]) + wide(near[1]) + wide(near[2]) + wide(partner)


def stratum_kernel(
    stratum, me, step, row_pick, col_pick, count, *refs
):
    u_in, (v_in, tiles, noise) = refs[:PEERS], refs[PEERS : PEERS + 3]
    q_out, v_out = refs[PEERS + 3 : 2 * PEERS + 3], refs[2 * PEERS + 3]
    u_s, v_s, t_s, n_s, r_acc, c_acc, q_s, u_sem, v_sem, t_sem, n_sem, o_sem = refs[2 * PEERS + 4 :]
    n_col = v_s.shape[0]
    n_slot = t_s.shape[0]
    loads = [pltpu.make_async_copy(u_in[k], u_s.at[k], u_sem.at[k]) for k in range(PEERS)]
    loads += [
        pltpu.make_async_copy(v_in.at[pl.ds(c * TILE, TILE)], v_s.at[c], v_sem.at[c])
        for c in range(n_col)
    ]
    tile_loads = [
        pltpu.make_async_copy(tiles.at[stratum, 0, 0, t], t_s.at[t], t_sem.at[t])
        for t in range(n_slot)
    ]
    noise_loads = [
        pltpu.make_async_copy(noise.at[stratum, pl.ds(c * TILE, TILE)], n_s.at[c], n_sem.at[c])
        for c in range(n_col)
    ]
    for copy in loads + tile_loads + noise_loads:
        copy.start()
    r_acc[...] = jnp.zeros_like(r_acc)
    c_acc[...] = jnp.zeros_like(c_acc)
    for copy in loads + tile_loads:
        copy.wait()

    def slot(t, carry):
        r = row_pick[stratum, 0, 0, t] ^ me[0]
        c = col_pick[stratum, 0, 0, t]
        u = u_s[r]
        v = v_s[c]
        predicted = lax.dot_general(
            u, v, (((1,), (1,)), ((), ())), preferred_element_type=jnp.float32
        )
        residual = (t_s[t].astype(jnp.float32) - predicted).astype(jnp.bfloat16)
        r_acc[r] += jnp.dot(residual, v, preferred_element_type=jnp.float32)
        c_acc[c] += lax.dot_general(
            residual, u, (((0,), (0,)), ((), ())), preferred_element_type=jnp.float32
        )
        return carry

    lax.fori_loop(0, count[stratum, 0, 0], slot, 0)
    stores = []
    for k in range(PEERS):
        q_s[k] = r_acc[k].astype(jnp.bfloat16)
        stores.append(pltpu.make_async_copy(q_s.at[k], q_out[k], o_sem.at[k]))
        stores[-1].start()
    h = step[stratum]
    root = jnp.sqrt(jnp.full((1, 1), h, jnp.float32))
    for c in range(n_col):
        noise_loads[c].wait()
        current = v_s[c].astype(jnp.float32)
        moved = (
            current
            + (0.5 * h) * (c_acc[c] - prior_precision * current)
            + root * n_s[c].astype(jnp.float32)
        )
        v_s[c] = moved.astype(jnp.bfloat16)
        stores.append(
            pltpu.make_async_copy(v_s.at[c], v_out.at[pl.ds(c * TILE, TILE)], o_sem.at[PEERS + c])
        )
        stores[-1].start()
    for copy in stores:
        copy.wait()


def stratum_step(stratum, me, step_sizes, tile_rows, tile_cols, tile_counts, rows, panel, tiles, noise):
    rank = panel.shape[1]
    n_col = panel.shape[0] // TILE
    n_slot = tiles.shape[3]
    smem = pl.BlockSpec(memory_space=pltpu.SMEM)
    any_space = pl.BlockSpec(memory_space=pl.ANY)
    part = jax.ShapeDtypeStruct((TILE, rank), jnp.bfloat16)
    out = pl.pallas_call(
        functools.partial(stratum_kernel, stratum),
        out_shape=[part] * PEERS + [jax.ShapeDtypeStruct(panel.shape, jnp.bfloat16)],
        in_specs=[smem] * 5 + [any_space] * (PEERS + 3),
        out_specs=[any_space] * (PEERS + 1),
        scratch_shapes=[
            pltpu.VMEM((PEERS, TILE, rank), jnp.bfloat16),
            pltpu.VMEM((n_col, TILE, rank), jnp.bfloat16),
            pltpu.VMEM((n_slot, TILE, TILE), jnp.bfloat16),
            pltpu.VMEM((n_col, TILE, rank), jnp.bfloat16),
            pltpu.VMEM((PEERS, TILE, rank), jnp.float32),
            pltpu.VMEM((n_col, TILE, rank), jnp.float32),
            pltpu.VMEM((PEERS, TILE, rank), jnp.bfloat16),
            pltpu.SemaphoreType.DMA((PEERS,)),
            pltpu.SemaphoreType.DMA((n_col,)),
            pltpu.SemaphoreType.DMA((n_slot,)),
            pltpu.SemaphoreType.DMA((n_col,)),
            pltpu.SemaphoreType.DMA((PEERS + n_col,)),
        ],
        compiler_params=pltpu.CompilerParams(vmem_limit_bytes=32 * 1024 * 1024),
        cost_estimate=pl.CostEstimate(
            flops=6 * n_slot * TILE * TILE * rank, bytes_accessed=9 << 20, transcendentals=0
        ),
        name="stratum_%d" % stratum,
    )(me, step_sizes, tile_rows, tile_cols, tile_counts, *rows, panel, tiles, noise)
    return out[:PEERS], out[PEERS]


def on_device(
    row_factor,
    col_factor,
    tiles,
    tile_rows,
    tile_cols,
    tile_counts,
    matching,
    row_noise,
    col_noise,
    step_sizes,
):
    me = lax.axis_index("cols").astype(jnp.int32).reshape(1)
    first = matching[0, 0]
    blocks = lax.axis_size("rows")

    def move(mask, panel):
        return swap(panel, "rows", mask) if mask else panel

    rows = gather_rows(row_factor)
    panel = lax.switch(first, [functools.partial(move, k) for k in range(blocks)], col_factor)
    parts, panel = stratum_step(
        0, me, step_sizes, tile_rows, tile_cols, tile_counts, rows, panel, tiles, col_noise
    )
    panel = swap(panel, "rows", blocks - 1)
    shard = langevin(row_factor, scatter_rows(parts), row_noise[0], step_sizes[0])
    shard = shard.astype(jnp.bfloat16)
    rows = gather_rows(shard)
    parts, panel = stratum_step(
        1, me, step_sizes, tile_rows, tile_cols, tile_counts, rows, panel, tiles, col_noise
    )
    home = lax.switch(
        first, [functools.partial(move, k ^ (blocks - 1)) for k in range(blocks)], panel
    )
    shard = langevin(shard, scatter_rows(parts), row_noise[1], step_sizes[1])
    return shard.astype(jnp.bfloat16), home


def solution(mesh):
    return jax.shard_map(
        on_device,
        mesh=mesh,
        in_specs=(
            P(("rows", "cols"), None),
            P(("rows", "cols"), None),
            P(None, "rows", "cols", None, None, None),
            P(None, "rows", "cols", None),
            P(None, "rows", "cols", None),
            P(None, "rows", "cols"),
            P(),
            P(None, ("rows", "cols"), None),
            P(None, ("rows", "cols"), None),
            P(),
        ),
        out_specs=(P(("rows", "cols"), None), P(("rows", "cols"), None)),
        check_vma=False,
    )
```

```python
import functools

import jax
import jax.numpy as jnp
from jax import lax
from jax.experimental import pallas as pl
from jax.experimental.pallas import tpu as pltpu
from jax.sharding import PartitionSpec as P

TILE = 256
PEERS = 8
GROUP = 4

prior_precision = 1.0


def swap(value, axis, mask):
    return lax.ppermute(value, axis, [(i, i ^ mask) for i in range(lax.axis_size(axis))])


def langevin(current, gradient, gaussian, step_size):
    current_wide = current.astype(jnp.float32)
    return (
        current_wide
        + 0.5 * step_size * (gradient - prior_precision * current_wide)
        + jnp.sqrt(step_size) * gaussian.astype(jnp.float32)
    )


def wide(value):
    return value.astype(jnp.float32)


def after(value, *others):
    return lax.optimization_barrier((value,) + others)[0]


def swap_near(parts, base):
    pick = (lambda k: parts[base + k]) if isinstance(parts, (list, tuple)) else (lambda k: parts)
    return [swap(pick(k), "cols", k) for k in (1, 2, 3)]


def stratum_kernel(stratum, me, step, row_pick, col_pick, count, *refs):
    u_in, (va_in, vb_in, tiles, noise) = refs[:PEERS], refs[PEERS : PEERS + 4]
    q_out, (va_out, vb_out) = refs[PEERS + 4 : 2 * PEERS + 4], refs[2 * PEERS + 4 : 2 * PEERS + 6]
    u_s, v_s, t_s, n_s, r_acc, c_acc, q_s, u_sem, v_sem, t_sem, n_sem, o_sem = refs[2 * PEERS + 6 :]
    n_col, rank = v_s.shape[0], v_s.shape[2]
    half = n_col // 2
    n_group = t_s.shape[0] // GROUP
    loads = [pltpu.make_async_copy(u_in[k], u_s.at[k], u_sem.at[k]) for k in range(PEERS)]
    for i, v_in in enumerate((va_in, vb_in)):
        loads.append(
            pltpu.make_async_copy(
                v_in.reshape(half, TILE, rank), v_s.at[pl.ds(i * half, half)], v_sem.at[i]
            )
        )

    def tile_load(i):
        span = pl.ds(i * GROUP, GROUP)
        return pltpu.make_async_copy(tiles.at[stratum, 0, 0, span], t_s.at[span], t_sem.at[i])

    noise_load = pltpu.make_async_copy(
        noise.at[stratum].reshape(n_col, TILE, rank), n_s, n_sem.at[0]
    )
    for copy in loads:
        copy.start()
    for i in range(n_group):
        tile_load(i).start()
    noise_load.start()
    r_acc[...] = jnp.zeros_like(r_acc)
    c_acc[...] = jnp.zeros_like(c_acc)
    for copy in loads:
        copy.wait()
    total = count[stratum, 0, 0]

    def group(i, carry):
        tile_load(i).wait()
        work = []
        for j in range(GROUP):
            t = i * GROUP + j
            r = row_pick[stratum, 0, 0, t] ^ me[0]
            c = col_pick[stratum, 0, 0, t]
            predicted = lax.dot_general(
                u_s[r], v_s[c], (((1,), (1,)), ((), ())), preferred_element_type=jnp.float32
            )
            residual = (wide(t_s[t]) - predicted).astype(jnp.bfloat16)
            work.append((r, c, jnp.where(t < total, residual, jnp.zeros_like(residual))))
        for r, c, residual in work:
            r_acc[r] += jnp.dot(residual, v_s[c], preferred_element_type=jnp.float32)
            c_acc[c] += lax.dot_general(
                residual, u_s[r], (((0,), (0,)), ((), ())), preferred_element_type=jnp.float32
            )
        return carry

    def unused(i, carry):
        tile_load(i).wait()
        return carry

    used = (total + GROUP - 1) // GROUP
    lax.fori_loop(0, used, group, 0)
    lax.fori_loop(used, n_group, unused, 0)
    stores = []
    for k in (5, 6, 7, 4, 1, 2, 3, 0):
        q_s[k] = r_acc[k].astype(jnp.bfloat16)
        stores.append(pltpu.make_async_copy(q_s.at[k], q_out[k], o_sem.at[k]))
        stores[-1].start()
    h = step[stratum]
    root = jnp.sqrt(jnp.full((1, 1), h, jnp.float32))
    noise_load.wait()
    for i, v_out in enumerate((va_out, vb_out)):
        for c in range(i * half, (i + 1) * half):
            current = wide(v_s[c])
            moved = (
                current + (0.5 * h) * (c_acc[c] - prior_precision * current) + root * wide(n_s[c])
            )
            v_s[c] = moved.astype(jnp.bfloat16)
        stores.append(
            pltpu.make_async_copy(
                v_s.at[pl.ds(i * half, half)], v_out.reshape(half, TILE, rank), o_sem.at[PEERS + i]
            )
        )
        stores[-1].start()
    for copy in stores:
        copy.wait()


def stratum_step(stratum, me, step_sizes, tile_rows, tile_cols, tile_counts, rows, halves, tiles, noise):
    rank = noise.shape[2]
    n_col = noise.shape[1] // TILE
    n_slot = tiles.shape[3]
    smem = pl.BlockSpec(memory_space=pltpu.SMEM)
    free = pl.BlockSpec(memory_space=pl.ANY)
    hbm = pl.BlockSpec(memory_space=pltpu.HBM)
    part = jax.ShapeDtypeStruct((TILE, rank), jnp.bfloat16)
    half = jax.ShapeDtypeStruct(halves[0].shape, jnp.bfloat16)
    out = pl.pallas_call(
        functools.partial(stratum_kernel, stratum),
        out_shape=[part] * PEERS + [half] * 2,
        in_specs=[smem] * 5 + [free] * (PEERS + 2) + [hbm] * 2,
        out_specs=[free] * (PEERS + 2),
        scratch_shapes=[
            pltpu.VMEM((PEERS, TILE, rank), jnp.bfloat16),
            pltpu.VMEM((n_col, TILE, rank), jnp.bfloat16),
            pltpu.VMEM((n_slot, TILE, TILE), jnp.bfloat16),
            pltpu.VMEM((n_col, TILE, rank), jnp.bfloat16),
            pltpu.VMEM((PEERS, TILE, rank), jnp.float32),
            pltpu.VMEM((n_col, TILE, rank), jnp.float32),
            pltpu.VMEM((PEERS, TILE, rank), jnp.bfloat16),
            pltpu.SemaphoreType.DMA((PEERS,)),
            pltpu.SemaphoreType.DMA((2,)),
            pltpu.SemaphoreType.DMA((n_slot // GROUP,)),
            pltpu.SemaphoreType.DMA((1,)),
            pltpu.SemaphoreType.DMA((PEERS + 2,)),
        ],
        compiler_params=pltpu.CompilerParams(vmem_limit_bytes=32 * 1024 * 1024),
        cost_estimate=pl.CostEstimate(
            flops=6 * n_slot * TILE * TILE * rank, bytes_accessed=9 << 20, transcendentals=0
        ),
        name="stratum_%d" % stratum,
    )(me, step_sizes, tile_rows, tile_cols, tile_counts, *rows, *halves, tiles, noise)
    return out[:PEERS], out[PEERS:]


def on_device(
    row_factor,
    col_factor,
    tiles,
    tile_rows,
    tile_cols,
    tile_counts,
    matching,
    row_noise,
    col_noise,
    step_sizes,
):
    me = lax.axis_index("cols").astype(jnp.int32).reshape(1)
    blocks = lax.axis_size("rows")
    first = matching[0, 0]
    half = col_factor.shape[0] // 2

    def enter(mask, low, panel):
        piece = panel[low : low + half]
        return swap(piece, "rows", mask) if mask else piece

    def leave(mask, piece):
        return swap(piece, "rows", mask) if mask else piece

    def route(branch, flip, *operands):
        return lax.switch(
            first, [functools.partial(branch, k ^ flip) for k in range(blocks)], *operands
        )

    def kernel(stratum, rows, halves):
        return stratum_step(
            stratum, me, step_sizes, tile_rows, tile_cols, tile_counts, rows, halves, tiles, col_noise
        )

    partner = swap(row_factor, "cols", 4)
    near = swap_near(row_factor, 0)
    upper = route(lambda k, v: enter(k, 0, v), 0, col_factor)
    partner, upper, near = lax.optimization_barrier((partner, upper, near))
    far = swap_near(partner, 0)
    lower = route(lambda k, v: enter(k, half, v), 0, after(col_factor, partner))
    parts, halves = kernel(0, [row_factor] + near + [partner] + far, (upper, lower))

    far = swap_near(parts, 4)
    upper = swap(halves[0], "rows", blocks - 1)
    near = swap_near(parts, 0)
    far_sum = wide(parts[4]) + wide(far[0]) + wide(far[1]) + wide(far[2])
    partner = swap(far_sum.astype(jnp.bfloat16), "cols", 4)
    partner, upper = lax.optimization_barrier((partner, upper))
    total = wide(parts[0]) + wide(near[0]) + wide(near[1]) + wide(near[2]) + wide(partner)
    shard = langevin(row_factor, total, row_noise[0], step_sizes[0]).astype(jnp.bfloat16)

    partner = swap(shard, "cols", 4)
    near = swap_near(shard, 0)
    far = swap_near(partner, 0)
    lower = swap(after(halves[1], partner), "rows", blocks - 1)
    parts, halves = kernel(1, [shard] + near + [partner] + far, (upper, lower))

    far = swap_near(parts, 4)
    near = swap_near(parts, 0)
    upper = route(leave, blocks - 1, halves[0])
    far_sum = wide(parts[4]) + wide(far[0]) + wide(far[1]) + wide(far[2])
    far_sum, upper = lax.optimization_barrier((far_sum.astype(jnp.bfloat16), upper))
    partner = swap(far_sum, "cols", 4)
    lower = route(leave, blocks - 1, after(halves[1], far_sum))
    total = wide(parts[0]) + wide(near[0]) + wide(near[1]) + wide(near[2]) + wide(partner)
    row_sample = langevin(shard, total, row_noise[1], step_sizes[1]).astype(jnp.bfloat16)
    return row_sample, jnp.concatenate([upper, lower], axis=0)


def solution(mesh):
    return jax.shard_map(
        on_device,
        mesh=mesh,
        in_specs=(
            P(("rows", "cols"), None),
            P(("rows", "cols"), None),
            P(None, "rows", "cols", None, None, None),
            P(None, "rows", "cols", None),
            P(None, "rows", "cols", None),
            P(None, "rows", "cols"),
            P(),
            P(None, ("rows", "cols"), None),
            P(None, ("rows", "cols"), None),
            P(),
        ),
        out_specs=(P(("rows", "cols"), None), P(("rows", "cols"), None)),
        check_vma=False,
    )
```

```python
import functools

import jax
import jax.numpy as jnp
from jax import lax
from jax.experimental import pallas as pl
from jax.experimental.pallas import tpu as pltpu
from jax.sharding import PartitionSpec as P

TILE = 256
PEERS = 8
GROUP = 4

prior_precision = 1.0


def swap(value, axis, mask):
    return lax.ppermute(value, axis, [(i, i ^ mask) for i in range(lax.axis_size(axis))])


def langevin(current, gradient, gaussian, step_size):
    current_wide = current.astype(jnp.float32)
    return (
        current_wide
        + 0.5 * step_size * (gradient - prior_precision * current_wide)
        + jnp.sqrt(step_size) * gaussian.astype(jnp.float32)
    )


def wide(value):
    return value.astype(jnp.float32)


def after(value, *others):
    return lax.optimization_barrier((value,) + others)[0]


def swap_near(parts, base):
    pick = (lambda k: parts[base + k]) if isinstance(parts, (list, tuple)) else (lambda k: parts)
    return [swap(pick(k), "cols", k) for k in (1, 2, 3)]


def stratum_kernel(stratum, me, step, row_pick, col_pick, count, *refs):
    u_in, (va_in, vb_in, tiles, noise) = refs[:PEERS], refs[PEERS : PEERS + 4]
    q_out, (va_out, vb_out) = refs[PEERS + 4 : 2 * PEERS + 4], refs[2 * PEERS + 4 : 2 * PEERS + 6]
    u_s, v_s, t_s, n_s, r_acc, c_acc, q_s, u_sem, v_sem, t_sem, n_sem, o_sem = refs[2 * PEERS + 6 :]
    n_group = t_s.shape[0] // GROUP
    cut = va_in.shape[0]
    spans = (pl.ds(0, cut), pl.ds(cut, v_s.shape[0] - cut))
    loads = [pltpu.make_async_copy(u_in[k], u_s.at[k], u_sem.at[k]) for k in range(PEERS)]
    for i, v_in in enumerate((va_in, vb_in)):
        loads.append(pltpu.make_async_copy(v_in, v_s.at[spans[i]], v_sem.at[i]))

    def tile_load(i):
        span = pl.ds(i * GROUP, GROUP)
        return pltpu.make_async_copy(tiles.at[stratum, 0, 0, span], t_s.at[span], t_sem.at[i])

    noise_load = pltpu.make_async_copy(noise.at[stratum], n_s, n_sem.at[0])
    for copy in loads:
        copy.start()
    for i in range(n_group):
        tile_load(i).start()
    noise_load.start()
    r_acc[...] = jnp.zeros_like(r_acc)
    c_acc[...] = jnp.zeros_like(c_acc)
    for copy in loads:
        copy.wait()
    total = count[stratum, 0, 0]

    def group(i, carry):
        tile_load(i).wait()
        work = []
        for j in range(GROUP):
            t = i * GROUP + j
            r = row_pick[stratum, 0, 0, t] ^ me[0]
            c = pl.ds(pl.multiple_of(col_pick[stratum, 0, 0, t] * TILE, TILE), TILE)
            predicted = lax.dot_general(
                u_s[r], v_s[c], (((1,), (1,)), ((), ())), preferred_element_type=jnp.float32
            )
            residual = (wide(t_s[t]) - predicted).astype(jnp.bfloat16)
            work.append((r, c, jnp.where(t < total, residual, jnp.zeros_like(residual))))
        for r, c, residual in work:
            r_acc[r] += jnp.dot(residual, v_s[c], preferred_element_type=jnp.float32)
            c_acc[c] += lax.dot_general(
                residual, u_s[r], (((0,), (0,)), ((), ())), preferred_element_type=jnp.float32
            )
        return carry

    def unused(i, carry):
        tile_load(i).wait()
        return carry

    used = (total + GROUP - 1) // GROUP
    lax.fori_loop(0, used, group, 0)
    lax.fori_loop(used, n_group, unused, 0)
    stores = []
    for k in (5, 6, 7, 4, 1, 2, 3, 0):
        q_s[k] = r_acc[k].astype(jnp.bfloat16)
        stores.append(pltpu.make_async_copy(q_s.at[k], q_out[k], o_sem.at[k]))
        stores[-1].start()
    h = step[stratum]
    root = jnp.sqrt(jnp.full((1, 1), h, jnp.float32))
    noise_load.wait()
    for i, v_out in enumerate((va_out, vb_out)):
        for low in range(spans[i].start, spans[i].start + spans[i].size, TILE // 2):
            rows = pl.ds(low, TILE // 2)
            current = wide(v_s[rows])
            moved = (
                current
                + (0.5 * h) * (c_acc[rows] - prior_precision * current)
                + root * wide(n_s[rows])
            )
            v_s[rows] = moved.astype(jnp.bfloat16)
        stores.append(pltpu.make_async_copy(v_s.at[spans[i]], v_out, o_sem.at[PEERS + i]))
        stores[-1].start()
    for copy in stores:
        copy.wait()


def stratum_step(stratum, me, step_sizes, tile_rows, tile_cols, tile_counts, rows, halves, tiles, noise):
    n_col, rank = noise.shape[1:]
    n_slot = tiles.shape[3]
    smem = pl.BlockSpec(memory_space=pltpu.SMEM)
    free = pl.BlockSpec(memory_space=pl.ANY)
    part = jax.ShapeDtypeStruct((TILE, rank), jnp.bfloat16)
    out = pl.pallas_call(
        functools.partial(stratum_kernel, stratum),
        out_shape=[part] * PEERS
        + [jax.ShapeDtypeStruct(v.shape, jnp.bfloat16) for v in halves],
        in_specs=[smem] * 5 + [free] * (PEERS + 4),
        out_specs=[free] * (PEERS + 2),
        scratch_shapes=[
            pltpu.VMEM((PEERS, TILE, rank), jnp.bfloat16),
            pltpu.VMEM((n_col, rank), jnp.bfloat16),
            pltpu.VMEM((n_slot, TILE, TILE), jnp.bfloat16),
            pltpu.VMEM((n_col, rank), jnp.bfloat16),
            pltpu.VMEM((PEERS, TILE, rank), jnp.float32),
            pltpu.VMEM((n_col, rank), jnp.float32),
            pltpu.VMEM((PEERS, TILE, rank), jnp.bfloat16),
            pltpu.SemaphoreType.DMA((PEERS,)),
            pltpu.SemaphoreType.DMA((2,)),
            pltpu.SemaphoreType.DMA((n_slot // GROUP,)),
            pltpu.SemaphoreType.DMA((1,)),
            pltpu.SemaphoreType.DMA((PEERS + 2,)),
        ],
        compiler_params=pltpu.CompilerParams(vmem_limit_bytes=46 * 1024 * 1024),
        cost_estimate=pl.CostEstimate(
            flops=6 * n_slot * TILE * TILE * rank, bytes_accessed=9 << 20, transcendentals=0
        ),
        name="stratum_%d" % stratum,
    )(me, step_sizes, tile_rows, tile_cols, tile_counts, *rows, *halves, tiles, noise)
    return out[:PEERS], out[PEERS:]


def finish_kernel(step, *refs):
    part_in, (shard, noise, va_in, vb_in) = refs[:5], refs[5:9]
    row_out, col_out, part_s, own_s, sem, col_sem = refs[9:]
    stratum = noise.shape[0] - 1
    cut = va_in.shape[0]
    copies = [
        pltpu.make_async_copy(va_in, col_out.at[pl.ds(0, cut)], col_sem.at[0]),
        pltpu.make_async_copy(
            vb_in, col_out.at[pl.ds(cut, vb_in.shape[0])], col_sem.at[1]
        ),
    ]
    loads = [pltpu.make_async_copy(part_in[i], part_s.at[i], sem.at[i]) for i in range(5)]
    loads.append(pltpu.make_async_copy(shard, own_s.at[0], sem.at[5]))
    loads.append(pltpu.make_async_copy(noise.at[stratum], own_s.at[1], sem.at[6]))
    for copy in copies + loads:
        copy.start()
    for copy in loads:
        copy.wait()
    total = wide(part_s[0]) + wide(part_s[1]) + wide(part_s[2]) + wide(part_s[3]) + wide(part_s[4])
    h = step[stratum]
    root = jnp.sqrt(jnp.full((1, 1), h, jnp.float32))
    current = wide(own_s[0])
    moved = current + (0.5 * h) * (total - prior_precision * current) + root * wide(own_s[1])
    row_out[...] = moved.astype(jnp.bfloat16)
    for copy in copies:
        copy.wait()


def finish(step_sizes, terms, shard, row_noise, upper, lower):
    free = pl.BlockSpec(memory_space=pl.ANY)
    panel = (upper.shape[0] + lower.shape[0], upper.shape[1])
    return pl.pallas_call(
        finish_kernel,
        out_shape=[
            jax.ShapeDtypeStruct(shard.shape, jnp.bfloat16),
            jax.ShapeDtypeStruct(panel, jnp.bfloat16),
        ],
        in_specs=[pl.BlockSpec(memory_space=pltpu.SMEM)] + [free] * 9,
        out_specs=[pl.BlockSpec(memory_space=pltpu.VMEM), free],
        scratch_shapes=[
            pltpu.VMEM((5,) + shard.shape, jnp.bfloat16),
            pltpu.VMEM((2,) + shard.shape, jnp.bfloat16),
            pltpu.SemaphoreType.DMA((7,)),
            pltpu.SemaphoreType.DMA((2,)),
        ],
        compiler_params=pltpu.CompilerParams(vmem_limit_bytes=16 * 1024 * 1024),
        name="finish",
    )(step_sizes, *terms, shard, row_noise, upper, lower)


def on_device(
    row_factor,
    col_factor,
    tiles,
    tile_rows,
    tile_cols,
    tile_counts,
    matching,
    row_noise,
    col_noise,
    step_sizes,
):
    me = lax.axis_index("cols").astype(jnp.int32).reshape(1)
    blocks = lax.axis_size("rows")
    first = matching[0, 0]
    cut = col_factor.shape[0] * 3 // 8

    def enter(mask, span, panel):
        piece = panel[span]
        return swap(piece, "rows", mask) if mask else piece

    def leave(mask, piece):
        return swap(piece, "rows", mask) if mask else piece

    def route(branch, flip, *operands):
        return lax.switch(
            first, [functools.partial(branch, k ^ flip) for k in range(blocks)], *operands
        )

    def kernel(stratum, rows, halves):
        return stratum_step(
            stratum, me, step_sizes, tile_rows, tile_cols, tile_counts, rows, halves, tiles, col_noise
        )

    partner = swap(row_factor, "cols", 4)
    near = swap_near(row_factor, 0)
    upper = route(lambda k, v: enter(k, slice(0, cut), v), 0, col_factor)
    partner, upper, near = lax.optimization_barrier((partner, upper, near))
    far = swap_near(partner, 0)
    lower = route(lambda k, v: enter(k, slice(cut, None), v), 0, after(col_factor, partner))
    parts, halves = kernel(0, [row_factor] + near + [partner] + far, (upper, lower))

    far = swap_near(parts, 4)
    upper = swap(halves[0], "rows", blocks - 1)
    near = swap_near(parts, 0)
    far_sum = wide(parts[4]) + wide(far[0]) + wide(far[1]) + wide(far[2])
    partner = swap(far_sum.astype(jnp.bfloat16), "cols", 4)
    partner, upper = lax.optimization_barrier((partner, upper))
    total = wide(parts[0]) + wide(near[0]) + wide(near[1]) + wide(near[2]) + wide(partner)
    shard = langevin(row_factor, total, row_noise[0], step_sizes[0]).astype(jnp.bfloat16)

    partner = swap(shard, "cols", 4)
    near = swap_near(shard, 0)
    partner, near = lax.optimization_barrier((partner, near))
    far = swap_near(partner, 0)
    lower = swap(after(halves[1], partner), "rows", blocks - 1)
    parts, halves = kernel(1, [shard] + near + [partner] + far, (upper, lower))

    far = swap_near(parts, 4)
    upper = route(leave, blocks - 1, halves[0])
    far_sum = wide(parts[4]) + wide(far[0]) + wide(far[1]) + wide(far[2])
    far_sum, upper = lax.optimization_barrier((far_sum.astype(jnp.bfloat16), upper))
    partner = swap(far_sum, "cols", 4)
    near = swap_near([after(part, far_sum) for part in parts[:4]], 0)
    lower = route(leave, blocks - 1, after(halves[1], far_sum))
    return finish(step_sizes, [parts[0]] + near + [partner], shard, row_noise, upper, lower)


def solution(mesh):
    return jax.shard_map(
        on_device,
        mesh=mesh,
        in_specs=(
            P(("rows", "cols"), None),
            P(("rows", "cols"), None),
            P(None, "rows", "cols", None, None, None),
            P(None, "rows", "cols", None),
            P(None, "rows", "cols", None),
            P(None, "rows", "cols"),
            P(),
            P(None, ("rows", "cols"), None),
            P(None, ("rows", "cols"), None),
            P(),
        ),
        out_specs=(P(("rows", "cols"), None), P(("rows", "cols"), None)),
        check_vma=False,
    )
```

```python
import functools

import jax
import jax.numpy as jnp
from jax import lax
from jax.experimental import pallas as pl
from jax.experimental.pallas import tpu as pltpu
from jax.sharding import PartitionSpec as P

TILE = 256
PEERS = 8
GROUP = 4

prior_precision = 1.0


def swap(value, axis, mask):
    return lax.ppermute(value, axis, [(i, i ^ mask) for i in range(lax.axis_size(axis))])


def langevin(current, gradient, gaussian, step_size):
    current_wide = current.astype(jnp.float32)
    return (
        current_wide
        + 0.5 * step_size * (gradient - prior_precision * current_wide)
        + jnp.sqrt(step_size) * gaussian.astype(jnp.float32)
    )


def wide(value):
    return value.astype(jnp.float32)


def after(value, *others):
    return lax.optimization_barrier((value,) + others)[0]


def swap_near(parts, base):
    pick = (lambda k: parts[base + k]) if isinstance(parts, (list, tuple)) else (lambda k: parts)
    return [swap(pick(k), "cols", k) for k in (1, 2, 3)]


def stratum_kernel(stratum, me, step, row_pick, col_pick, count, *refs):
    u_in, (va_in, vb_in, tiles, noise) = refs[:PEERS], refs[PEERS : PEERS + 4]
    q_out, (va_out, vb_out) = refs[PEERS + 4 : 2 * PEERS + 4], refs[2 * PEERS + 4 : 2 * PEERS + 6]
    u_s, v_s, t_s, n_s, r_acc, c_acc, q_s, u_sem, v_sem, t_sem, n_sem, o_sem = refs[2 * PEERS + 6 :]
    n_group = t_s.shape[0] // GROUP
    loads = [pltpu.make_async_copy(u_in[k], u_s.at[k], u_sem.at[k]) for k in range(PEERS)]
    for i, v_in in enumerate((va_in, vb_in)):
        span = pl.ds(i * va_in.shape[0], v_in.shape[0])
        loads.append(pltpu.make_async_copy(v_in, v_s.at[span], v_sem.at[i]))

    def tile_load(i):
        span = pl.ds(i * GROUP, GROUP)
        return pltpu.make_async_copy(tiles.at[stratum, 0, 0, span], t_s.at[span], t_sem.at[i])

    noise_load = pltpu.make_async_copy(noise.at[stratum], n_s, n_sem.at[0])
    for copy in loads:
        copy.start()
    for i in range(n_group):
        tile_load(i).start()
    noise_load.start()
    r_acc[...] = jnp.zeros_like(r_acc)
    c_acc[...] = jnp.zeros_like(c_acc)
    for copy in loads:
        copy.wait()
    total = count[stratum, 0, 0]

    def group(i, carry):
        tile_load(i).wait()
        work = []
        for j in range(GROUP):
            t = i * GROUP + j
            r = row_pick[stratum, 0, 0, t] ^ me[0]
            c = pl.ds(pl.multiple_of(col_pick[stratum, 0, 0, t] * TILE, TILE), TILE)
            predicted = lax.dot_general(
                u_s[r], v_s[c], (((1,), (1,)), ((), ())), preferred_element_type=jnp.float32
            )
            residual = (wide(t_s[t]) - predicted).astype(jnp.bfloat16)
            work.append((r, c, jnp.where(t < total, residual, jnp.zeros_like(residual))))
        for r, c, residual in work:
            r_acc[r] += jnp.dot(residual, v_s[c], preferred_element_type=jnp.float32)
            c_acc[c] += lax.dot_general(
                residual, u_s[r], (((0,), (0,)), ((), ())), preferred_element_type=jnp.float32
            )
        return carry

    def unused(i, carry):
        tile_load(i).wait()
        return carry

    used = (total + GROUP - 1) // GROUP
    lax.fori_loop(0, used, group, 0)
    lax.fori_loop(used, n_group, unused, 0)
    stores = []
    for k in (5, 6, 7, 4, 1, 2, 3, 0):
        q_s[k] = r_acc[k].astype(jnp.bfloat16)
        stores.append(pltpu.make_async_copy(q_s.at[k], q_out[k], o_sem.at[k]))
        stores[-1].start()
    h = step[stratum]
    root = jnp.sqrt(jnp.full((1, 1), h, jnp.float32))
    noise_load.wait()
    for i, v_out in enumerate((va_out, vb_out)):
        first = i * va_out.shape[0]
        for low in range(first, first + v_out.shape[0], TILE // 2):
            rows = pl.ds(low, TILE // 2)
            current = wide(v_s[rows])
            moved = (
                current
                + (0.5 * h) * (c_acc[rows] - prior_precision * current)
                + root * wide(n_s[rows])
            )
            v_s[rows] = moved.astype(jnp.bfloat16)
        span = pl.ds(first, v_out.shape[0])
        stores.append(pltpu.make_async_copy(v_s.at[span], v_out, o_sem.at[PEERS + i]))
        stores[-1].start()
    for copy in stores:
        copy.wait()


def stratum_step(stratum, me, step_sizes, tile_rows, tile_cols, tile_counts, rows, halves, cut, tiles, noise):
    n_col, rank = noise.shape[1:]
    n_slot = tiles.shape[3]
    smem = pl.BlockSpec(memory_space=pltpu.SMEM)
    free = pl.BlockSpec(memory_space=pl.ANY)
    part = jax.ShapeDtypeStruct((TILE, rank), jnp.bfloat16)
    out = pl.pallas_call(
        functools.partial(stratum_kernel, stratum),
        out_shape=[part] * PEERS
        + [jax.ShapeDtypeStruct((n, rank), jnp.bfloat16) for n in (cut, n_col - cut)],
        in_specs=[smem] * 5 + [free] * (PEERS + 4),
        out_specs=[free] * (PEERS + 2),
        scratch_shapes=[
            pltpu.VMEM((PEERS, TILE, rank), jnp.bfloat16),
            pltpu.VMEM((n_col, rank), jnp.bfloat16),
            pltpu.VMEM((n_slot, TILE, TILE), jnp.bfloat16),
            pltpu.VMEM((n_col, rank), jnp.bfloat16),
            pltpu.VMEM((PEERS, TILE, rank), jnp.float32),
            pltpu.VMEM((n_col, rank), jnp.float32),
            pltpu.VMEM((PEERS, TILE, rank), jnp.bfloat16),
            pltpu.SemaphoreType.DMA((PEERS,)),
            pltpu.SemaphoreType.DMA((2,)),
            pltpu.SemaphoreType.DMA((n_slot // GROUP,)),
            pltpu.SemaphoreType.DMA((1,)),
            pltpu.SemaphoreType.DMA((PEERS + 2,)),
        ],
        compiler_params=pltpu.CompilerParams(vmem_limit_bytes=48 * 1024 * 1024),
        cost_estimate=pl.CostEstimate(
            flops=6 * n_slot * TILE * TILE * rank, bytes_accessed=9 << 20, transcendentals=0
        ),
        name="stratum_%d" % stratum,
    )(me, step_sizes, tile_rows, tile_cols, tile_counts, *rows, *halves, tiles, noise)
    return out[:PEERS], out[PEERS:]


def finish_kernel(step, *refs):
    part_in, (shard, noise, va_in, vb_in) = refs[:5], refs[5:9]
    row_out, col_out, part_s, own_s, v_s, sem, col_sem = refs[9:]
    stratum = noise.shape[0] - 1
    cut = va_in.shape[0]
    spans = (pl.ds(0, cut), pl.ds(cut, vb_in.shape[0]))
    pieces = [
        pltpu.make_async_copy(v_in, v_s.at[span], col_sem.at[i])
        for i, (v_in, span) in enumerate(zip((va_in, vb_in), spans))
    ]
    stores = [
        pltpu.make_async_copy(v_s.at[span], col_out.at[span], col_sem.at[2 + i])
        for i, span in enumerate(spans)
    ]
    loads = [pltpu.make_async_copy(part_in[i], part_s.at[i], sem.at[i]) for i in range(5)]
    loads.append(pltpu.make_async_copy(shard, own_s.at[0], sem.at[5]))
    loads.append(pltpu.make_async_copy(noise.at[stratum], own_s.at[1], sem.at[6]))
    for copy in pieces + loads:
        copy.start()
    for piece, store in zip(pieces, stores):
        piece.wait()
        store.start()
    for copy in loads:
        copy.wait()
    total = wide(part_s[0]) + wide(part_s[1]) + wide(part_s[2]) + wide(part_s[3]) + wide(part_s[4])
    h = step[stratum]
    root = jnp.sqrt(jnp.full((1, 1), h, jnp.float32))
    current = wide(own_s[0])
    moved = current + (0.5 * h) * (total - prior_precision * current) + root * wide(own_s[1])
    row_out[...] = moved.astype(jnp.bfloat16)
    for store in stores:
        store.wait()


def finish(step_sizes, terms, shard, row_noise, upper, lower):
    free = pl.BlockSpec(memory_space=pl.ANY)
    panel = (upper.shape[0] + lower.shape[0], upper.shape[1])
    return pl.pallas_call(
        finish_kernel,
        out_shape=[
            jax.ShapeDtypeStruct(shard.shape, jnp.bfloat16),
            jax.ShapeDtypeStruct(panel, jnp.bfloat16),
        ],
        in_specs=[pl.BlockSpec(memory_space=pltpu.SMEM)] + [free] * 9,
        out_specs=[pl.BlockSpec(memory_space=pltpu.VMEM), free],
        scratch_shapes=[
            pltpu.VMEM((5,) + shard.shape, jnp.bfloat16),
            pltpu.VMEM((2,) + shard.shape, jnp.bfloat16),
            pltpu.VMEM(panel, jnp.bfloat16),
            pltpu.SemaphoreType.DMA((7,)),
            pltpu.SemaphoreType.DMA((4,)),
        ],
        compiler_params=pltpu.CompilerParams(vmem_limit_bytes=16 * 1024 * 1024),
        name="finish",
    )(step_sizes, *terms, shard, row_noise, upper, lower)


def on_device(
    row_factor,
    col_factor,
    tiles,
    tile_rows,
    tile_cols,
    tile_counts,
    matching,
    row_noise,
    col_noise,
    step_sizes,
):
    me = lax.axis_index("cols").astype(jnp.int32).reshape(1)
    blocks = lax.axis_size("rows")
    first = matching[0, 0]
    cut = col_factor.shape[0] * 3 // 8

    def enter(mask, span, panel):
        piece = panel[span]
        return swap(piece, "rows", mask) if mask else piece

    def leave(mask, piece):
        return swap(piece, "rows", mask) if mask else piece

    def route(branch, flip, *operands):
        return lax.switch(
            first, [functools.partial(branch, k ^ flip) for k in range(blocks)], *operands
        )

    def kernel(stratum, rows, halves, cut_out):
        return stratum_step(
            stratum,
            me,
            step_sizes,
            tile_rows,
            tile_cols,
            tile_counts,
            rows,
            halves,
            cut_out,
            tiles,
            col_noise,
        )

    partner = swap(row_factor, "cols", 4)
    near = swap_near(row_factor, 0)
    upper = route(lambda k, v: enter(k, slice(0, cut), v), 0, col_factor)
    partner, upper, near = lax.optimization_barrier((partner, upper, near))
    far = swap_near(partner, 0)
    lower = route(lambda k, v: enter(k, slice(cut, None), v), 0, after(col_factor, partner))
    parts, halves = kernel(0, [row_factor] + near + [partner] + far, (upper, lower), col_factor.shape[0] - cut)

    far = swap_near(parts, 4)
    upper = swap(halves[0], "rows", blocks - 1)
    far_sum = wide(parts[4]) + wide(far[0]) + wide(far[1]) + wide(far[2])
    far_sum = far_sum.astype(jnp.bfloat16)
    partner = swap(far_sum, "cols", 4)
    near = swap_near([after(part, far_sum) for part in parts[:4]], 0)
    partner, upper = lax.optimization_barrier((partner, upper))
    total = wide(parts[0]) + wide(near[0]) + wide(near[1]) + wide(near[2]) + wide(partner)
    shard = langevin(row_factor, total, row_noise[0], step_sizes[0]).astype(jnp.bfloat16)

    partner = swap(shard, "cols", 4)
    near = swap_near(shard, 0)
    partner, near = lax.optimization_barrier((partner, near))
    far = swap_near(partner, 0)
    lower = swap(after(halves[1], partner), "rows", blocks - 1)
    parts, halves = kernel(1, [shard] + near + [partner] + far, (upper, lower), cut)

    far = swap_near(parts, 4)
    upper = route(leave, blocks - 1, halves[0])
    far_sum = wide(parts[4]) + wide(far[0]) + wide(far[1]) + wide(far[2])
    far_sum, upper = lax.optimization_barrier((far_sum.astype(jnp.bfloat16), upper))
    partner = swap(far_sum, "cols", 4)
    near = swap_near([after(part, far_sum) for part in parts[:4]], 0)
    lower = route(leave, blocks - 1, after(halves[1], far_sum))
    return finish(step_sizes, [parts[0]] + near + [partner], shard, row_noise, upper, lower)


def solution(mesh):
    return jax.shard_map(
        on_device,
        mesh=mesh,
        in_specs=(
            P(("rows", "cols"), None),
            P(("rows", "cols"), None),
            P(None, "rows", "cols", None, None, None),
            P(None, "rows", "cols", None),
            P(None, "rows", "cols", None),
            P(None, "rows", "cols"),
            P(),
            P(None, ("rows", "cols"), None),
            P(None, ("rows", "cols"), None),
            P(),
        ),
        out_specs=(P(("rows", "cols"), None), P(("rows", "cols"), None)),
        check_vma=False,
    )
```

```python
import functools

import jax
import jax.numpy as jnp
from jax import lax
from jax.experimental import pallas as pl
from jax.experimental.pallas import tpu as pltpu
from jax.sharding import PartitionSpec as P

TILE = 256
PEERS = 8
GROUP = 4

prior_precision = 1.0


def swap(value, axis, mask):
    return lax.ppermute(value, axis, [(i, i ^ mask) for i in range(lax.axis_size(axis))])


def langevin(current, gradient, gaussian, step_size):
    current_wide = current.astype(jnp.float32)
    return (
        current_wide
        + 0.5 * step_size * (gradient - prior_precision * current_wide)
        + jnp.sqrt(step_size) * gaussian.astype(jnp.float32)
    )


def wide(value):
    return value.astype(jnp.float32)


def after(value, *others):
    return lax.optimization_barrier((value,) + others)[0]


def swap_near(parts, base):
    pick = (lambda k: parts[base + k]) if isinstance(parts, (list, tuple)) else (lambda k: parts)
    return [swap(pick(k), "cols", k) for k in (1, 2, 3)]


def pieces_of(refs):
    low = 0
    for piece in refs:
        yield low, piece
        low += piece.shape[0]


def stratum_kernel(stratum, n_in, n_out, me, step, row_pick, col_pick, count, tiles, noise, *refs):
    u_in, refs = refs[:PEERS], refs[PEERS:]
    v_in, refs = refs[:n_in], refs[n_in:]
    q_out, refs = refs[:PEERS], refs[PEERS:]
    v_out, refs = refs[:n_out], refs[n_out:]
    u_s, v_s, t_s, n_s, r_acc, c_acc, q_s, u_sem, v_sem, t_sem, n_sem, o_sem = refs
    n_group = t_s.shape[0] // GROUP
    loads = [pltpu.make_async_copy(u_in[k], u_s.at[k], u_sem.at[k]) for k in range(PEERS)]
    for i, (low, piece) in enumerate(pieces_of(v_in)):
        loads.append(pltpu.make_async_copy(piece, v_s.at[pl.ds(low, piece.shape[0])], v_sem.at[i]))

    def tile_load(i):
        span = pl.ds(i * GROUP, GROUP)
        return pltpu.make_async_copy(tiles.at[stratum, 0, 0, span], t_s.at[span], t_sem.at[i])

    noise_load = pltpu.make_async_copy(noise.at[stratum], n_s, n_sem.at[0])
    for copy in loads:
        copy.start()
    for i in range(n_group):
        tile_load(i).start()
    noise_load.start()
    r_acc[...] = jnp.zeros_like(r_acc)
    c_acc[...] = jnp.zeros_like(c_acc)
    for copy in loads:
        copy.wait()
    total = count[stratum, 0, 0]

    def group(i, carry):
        tile_load(i).wait()
        work = []
        for j in range(GROUP):
            t = i * GROUP + j
            r = row_pick[stratum, 0, 0, t] ^ me[0]
            c = pl.ds(pl.multiple_of(col_pick[stratum, 0, 0, t] * TILE, TILE), TILE)
            predicted = lax.dot_general(
                u_s[r], v_s[c], (((1,), (1,)), ((), ())), preferred_element_type=jnp.float32
            )
            residual = (wide(t_s[t]) - predicted).astype(jnp.bfloat16)
            work.append((r, c, jnp.where(t < total, residual, jnp.zeros_like(residual))))
        for r, c, residual in work:
            r_acc[r] += jnp.dot(residual, v_s[c], preferred_element_type=jnp.float32)
            c_acc[c] += lax.dot_general(
                residual, u_s[r], (((0,), (0,)), ((), ())), preferred_element_type=jnp.float32
            )
        return carry

    def unused(i, carry):
        tile_load(i).wait()
        return carry

    used = (total + GROUP - 1) // GROUP
    lax.fori_loop(0, used, group, 0)
    lax.fori_loop(used, n_group, unused, 0)
    stores = []
    for k in (5, 6, 7, 4, 1, 2, 3, 0):
        q_s[k] = r_acc[k].astype(jnp.bfloat16)
        stores.append(pltpu.make_async_copy(q_s.at[k], q_out[k], o_sem.at[k]))
        stores[-1].start()
    h = step[stratum]
    root = jnp.sqrt(jnp.full((1, 1), h, jnp.float32))
    noise_load.wait()
    for i, (first, piece) in enumerate(pieces_of(v_out)):
        for low in range(first, first + piece.shape[0], TILE // 2):
            rows = pl.ds(low, TILE // 2)
            current = wide(v_s[rows])
            moved = (
                current
                + (0.5 * h) * (c_acc[rows] - prior_precision * current)
                + root * wide(n_s[rows])
            )
            v_s[rows] = moved.astype(jnp.bfloat16)
        span = pl.ds(first, piece.shape[0])
        stores.append(pltpu.make_async_copy(v_s.at[span], piece, o_sem.at[PEERS + i]))
        stores[-1].start()
    for copy in stores:
        copy.wait()


def stratum_step(stratum, smem_args, tiles, noise, rows, pieces, sizes):
    n_col, rank = noise.shape[1:]
    n_slot = tiles.shape[3]
    smem = pl.BlockSpec(memory_space=pltpu.SMEM)
    free = pl.BlockSpec(memory_space=pl.ANY)
    part = jax.ShapeDtypeStruct((TILE, rank), jnp.bfloat16)
    out = pl.pallas_call(
        functools.partial(stratum_kernel, stratum, len(pieces), len(sizes)),
        out_shape=[part] * PEERS
        + [jax.ShapeDtypeStruct((size, rank), jnp.bfloat16) for size in sizes],
        in_specs=[smem] * 5 + [free] * (2 + PEERS + len(pieces)),
        out_specs=[free] * (PEERS + len(sizes)),
        scratch_shapes=[
            pltpu.VMEM((PEERS, TILE, rank), jnp.bfloat16),
            pltpu.VMEM((n_col, rank), jnp.bfloat16),
            pltpu.VMEM((n_slot, TILE, TILE), jnp.bfloat16),
            pltpu.VMEM((n_col, rank), jnp.bfloat16),
            pltpu.VMEM((PEERS, TILE, rank), jnp.float32),
            pltpu.VMEM((n_col, rank), jnp.float32),
            pltpu.VMEM((PEERS, TILE, rank), jnp.bfloat16),
            pltpu.SemaphoreType.DMA((PEERS,)),
            pltpu.SemaphoreType.DMA((len(pieces),)),
            pltpu.SemaphoreType.DMA((n_slot // GROUP,)),
            pltpu.SemaphoreType.DMA((1,)),
            pltpu.SemaphoreType.DMA((PEERS + len(sizes),)),
        ],
        compiler_params=pltpu.CompilerParams(vmem_limit_bytes=48 * 1024 * 1024),
        cost_estimate=pl.CostEstimate(
            flops=6 * n_slot * TILE * TILE * rank, bytes_accessed=9 << 20, transcendentals=0
        ),
        name="stratum_%d" % stratum,
    )(*smem_args, tiles, noise, *rows, *pieces)
    return out[:PEERS], out[PEERS:]


def copy_kernel(source, target, buffer, sem):
    load = pltpu.make_async_copy(source, buffer, sem.at[0])
    load.start()
    load.wait()
    store = pltpu.make_async_copy(buffer, target, sem.at[1])
    store.start()
    store.wait()


def copied(value):
    free = pl.BlockSpec(memory_space=pl.ANY)
    return pl.pallas_call(
        copy_kernel,
        out_shape=jax.ShapeDtypeStruct(value.shape, value.dtype),
        in_specs=[free],
        out_specs=free,
        scratch_shapes=[pltpu.VMEM(value.shape, value.dtype), pltpu.SemaphoreType.DMA((2,))],
        name="copied",
    )(value)


def finish_kernel(step, *refs):
    part_in, (shard, noise, v_in) = refs[:5], refs[5:8]
    row_out, col_out, part_s, own_s, v_s, sem = refs[8:]
    stratum = noise.shape[0] - 1
    panel_in = pltpu.make_async_copy(v_in, v_s, sem.at[7])
    panel_out = pltpu.make_async_copy(v_s, col_out, sem.at[8])
    loads = [pltpu.make_async_copy(part_in[i], part_s.at[i], sem.at[i]) for i in range(5)]
    loads.append(pltpu.make_async_copy(shard, own_s.at[0], sem.at[5]))
    loads.append(pltpu.make_async_copy(noise.at[stratum], own_s.at[1], sem.at[6]))
    panel_in.start()
    for copy in loads:
        copy.start()
    panel_in.wait()
    panel_out.start()
    for copy in loads:
        copy.wait()
    total = wide(part_s[0]) + wide(part_s[1]) + wide(part_s[2]) + wide(part_s[3]) + wide(part_s[4])
    h = step[stratum]
    root = jnp.sqrt(jnp.full((1, 1), h, jnp.float32))
    current = wide(own_s[0])
    moved = current + (0.5 * h) * (total - prior_precision * current) + root * wide(own_s[1])
    row_out[...] = moved.astype(jnp.bfloat16)
    panel_out.wait()


def finish(step_sizes, terms, shard, row_noise, panel):
    free = pl.BlockSpec(memory_space=pl.ANY)
    return pl.pallas_call(
        finish_kernel,
        out_shape=[jax.ShapeDtypeStruct(x.shape, jnp.bfloat16) for x in (shard, panel)],
        in_specs=[pl.BlockSpec(memory_space=pltpu.SMEM)] + [free] * 8,
        out_specs=[pl.BlockSpec(memory_space=pltpu.VMEM), free],
        scratch_shapes=[
            pltpu.VMEM((5,) + shard.shape, jnp.bfloat16),
            pltpu.VMEM((2,) + shard.shape, jnp.bfloat16),
            pltpu.VMEM(panel.shape, jnp.bfloat16),
            pltpu.SemaphoreType.DMA((9,)),
        ],
        compiler_params=pltpu.CompilerParams(vmem_limit_bytes=16 * 1024 * 1024),
        name="finish",
    )(step_sizes, *terms, shard, row_noise, panel)


def on_device(
    row_factor,
    col_factor,
    tiles,
    tile_rows,
    tile_cols,
    tile_counts,
    matching,
    row_noise,
    col_noise,
    step_sizes,
):
    me = lax.axis_index("cols").astype(jnp.int32).reshape(1)
    blocks = lax.axis_size("rows")
    first = matching[0, 0]
    height = col_factor.shape[0]
    early = height * 5 // 8

    def move(mask, panel):
        return swap(panel, "rows", mask) if mask else copied(panel)

    def route(branch, flip, *operands):
        return lax.switch(
            first, [functools.partial(branch, k ^ flip) for k in range(blocks)], *operands
        )

    def kernel(stratum, rows, pieces, sizes):
        smem_args = (me, step_sizes, tile_rows, tile_cols, tile_counts)
        return stratum_step(stratum, smem_args, tiles, col_noise, rows, pieces, sizes)

    def gather_rows(shard):
        partner = swap(shard, "cols", 4)
        near = swap_near(shard, 0)
        far = [swap(after(partner, near[k - 1]), "cols", k) for k in (1, 2, 3)]
        return [shard] + near + [partner] + far

    def scatter_rows(parts):
        far = swap_near(parts, 4)
        far_sum = wide(parts[4]) + wide(far[0]) + wide(far[1]) + wide(far[2])
        far_sum = far_sum.astype(jnp.bfloat16)
        partner = swap(far_sum, "cols", 4)
        near = swap_near([after(part, far_sum) for part in parts[:4]], 0)
        return [parts[0]] + near + [partner], far_sum

    rows = gather_rows(row_factor)
    panel = route(move, 0, after(col_factor, *rows[1:5]))
    parts, pieces = kernel(0, rows, [panel], [early, height - early])

    terms, _ = scatter_rows(parts)
    upper = swap(pieces[0], "rows", blocks - 1)
    terms[-1], upper = lax.optimization_barrier((terms[-1], upper))
    total = wide(terms[0]) + wide(terms[1]) + wide(terms[2]) + wide(terms[3]) + wide(terms[4])
    shard = langevin(row_factor, total, row_noise[0], step_sizes[0]).astype(jnp.bfloat16)
    rows = gather_rows(shard)
    lower = swap(after(pieces[1], rows[4]), "rows", blocks - 1)
    parts, pieces = kernel(1, rows, [upper, lower], [height])

    terms, far_sum = scatter_rows(parts)
    panel = route(move, blocks - 1, after(pieces[0], far_sum))
    terms[-1], panel = lax.optimization_barrier((terms[-1], panel))
    return finish(step_sizes, terms, shard, row_noise, panel)


def solution(mesh):
    return jax.shard_map(
        on_device,
        mesh=mesh,
        in_specs=(
            P(("rows", "cols"), None),
            P(("rows", "cols"), None),
            P(None, "rows", "cols", None, None, None),
            P(None, "rows", "cols", None),
            P(None, "rows", "cols", None),
            P(None, "rows", "cols"),
            P(),
            P(None, ("rows", "cols"), None),
            P(None, ("rows", "cols"), None),
            P(),
        ),
        out_specs=(P(("rows", "cols"), None), P(("rows", "cols"), None)),
        check_vma=False,
    )
```

```python
import functools

import jax
import jax.numpy as jnp
from jax import lax
from jax.experimental import pallas as pl
from jax.experimental.pallas import tpu as pltpu
from jax.sharding import PartitionSpec as P

TILE = 256
PEERS = 8
GROUP = 4

prior_precision = 1.0


def swap(value, axis, mask):
    return lax.ppermute(value, axis, [(i, i ^ mask) for i in range(lax.axis_size(axis))])


def is_inner(row):
    return (row >> 1 ^ row >> 2) & 1


def swap_mirror(value, inner):
    size = lax.axis_size("rows")
    pairs = [(i, i ^ size - 1) for i in range(size) if is_inner(i) == inner]
    return lax.ppermute(value, "rows", pairs)


def langevin(current, gradient, gaussian, step_size):
    current_wide = current.astype(jnp.float32)
    return (
        current_wide
        + 0.5 * step_size * (gradient - prior_precision * current_wide)
        + jnp.sqrt(step_size) * gaussian.astype(jnp.float32)
    )


def wide(value):
    return value.astype(jnp.float32)


def after(value, *others):
    return lax.optimization_barrier((value,) + others)[0]


def swap_near(parts, base):
    pick = (lambda k: parts[base + k]) if isinstance(parts, (list, tuple)) else (lambda k: parts)
    return [swap(pick(k), "cols", k) for k in (1, 2, 3)]


def stratum_kernel(stratum, n_in, me, step, row_pick, col_pick, count, tiles, noise, *refs):
    u_in, refs = refs[:PEERS], refs[PEERS:]
    v_in, refs = refs[:n_in], refs[n_in:]
    n_part = PEERS if n_in == 1 else PEERS // 2
    q_out, v_out, refs = refs[:n_part], refs[n_part], refs[n_part + 1 :]
    u_s, v_s, t_s, n_s, r_acc, c_acc, q_s, u_sem, v_sem, t_sem, n_sem, o_sem = refs
    n_group = t_s.shape[0] // GROUP
    loads = [pltpu.make_async_copy(u_in[k], u_s.at[k], u_sem.at[k]) for k in range(PEERS)]
    panel_loads = [pltpu.make_async_copy(panel, v_s, v_sem.at[0]) for panel in v_in]

    def tile_load(i):
        span = pl.ds(i * GROUP, GROUP)
        return pltpu.make_async_copy(tiles.at[stratum, 0, 0, span], t_s.at[span], t_sem.at[i])

    noise_load = pltpu.make_async_copy(noise.at[stratum], n_s, n_sem.at[0])
    if n_in == 1:
        panel_loads[0].start()
    else:
        for inner, copy in zip((1, 0), panel_loads):
            pl.when(me[1] == inner)(copy.start)
    for copy in loads:
        copy.start()
    for i in range(n_group):
        tile_load(i).start()
    noise_load.start()
    r_acc[...] = jnp.zeros_like(r_acc)
    c_acc[...] = jnp.zeros_like(c_acc)
    for copy in loads + panel_loads[:1]:
        copy.wait()
    total = count[stratum, 0, 0]

    def group(i, carry):
        tile_load(i).wait()
        work = []
        for j in range(GROUP):
            t = i * GROUP + j
            r = row_pick[stratum, 0, 0, t] ^ me[0]
            c = pl.ds(pl.multiple_of(col_pick[stratum, 0, 0, t] * TILE, TILE), TILE)
            predicted = lax.dot_general(
                u_s[r], v_s[c], (((1,), (1,)), ((), ())), preferred_element_type=jnp.float32
            )
            residual = (wide(t_s[t]) - predicted).astype(jnp.bfloat16)
            work.append((r, c, jnp.where(t < total, residual, jnp.zeros_like(residual))))
        for r, c, residual in work:
            r_acc[r] += jnp.dot(residual, v_s[c], preferred_element_type=jnp.float32)
            c_acc[c] += lax.dot_general(
                residual, u_s[r], (((0,), (0,)), ((), ())), preferred_element_type=jnp.float32
            )
        return carry

    def unused(i, carry):
        tile_load(i).wait()
        return carry

    used = (total + GROUP - 1) // GROUP
    lax.fori_loop(0, used, group, 0)
    lax.fori_loop(used, n_group, unused, 0)
    stores = []
    for k in (5, 6, 7, 4, 1, 2, 3, 0):
        q_s[k] = r_acc[k].astype(jnp.bfloat16)
        if n_in == 1:
            target = q_out[k]
        else:
            target = q_out[k % 4].at[pl.ds(k // 4 * TILE, TILE)]
        stores.append(pltpu.make_async_copy(q_s.at[k], target, o_sem.at[k]))
        stores[-1].start()
    h = step[stratum]
    root = jnp.sqrt(jnp.full((1, 1), h, jnp.float32))
    noise_load.wait()
    for low in range(0, v_s.shape[0], TILE):
        rows = pl.ds(low, TILE)
        current = wide(v_s[rows])
        moved = current + (0.5 * h) * (c_acc[rows] - prior_precision * current) + root * wide(n_s[rows])
        v_s[rows] = moved.astype(jnp.bfloat16)
        stores.append(pltpu.make_async_copy(v_s.at[rows], v_out.at[rows], o_sem.at[len(stores)]))
        stores[-1].start()
    for copy in stores:
        copy.wait()


def stratum_step(stratum, smem_args, tiles, noise, rows, panels):
    n_col, rank = noise.shape[1:]
    n_slot = tiles.shape[3]
    smem = pl.BlockSpec(memory_space=pltpu.SMEM)
    free = pl.BlockSpec(memory_space=pl.ANY)
    n_part = PEERS if len(panels) == 1 else PEERS // 2
    part = jax.ShapeDtypeStruct((PEERS // n_part * TILE, rank), jnp.bfloat16)
    out = pl.pallas_call(
        functools.partial(stratum_kernel, stratum, len(panels)),
        out_shape=[part] * n_part + [jax.ShapeDtypeStruct((n_col, rank), jnp.bfloat16)],
        in_specs=[smem] * 5 + [free] * (2 + PEERS + len(panels)),
        out_specs=[free] * (n_part + 1),
        scratch_shapes=[
            pltpu.VMEM((PEERS, TILE, rank), jnp.bfloat16),
            pltpu.VMEM((n_col, rank), jnp.bfloat16),
            pltpu.VMEM((n_slot, TILE, TILE), jnp.bfloat16),
            pltpu.VMEM((n_col, rank), jnp.bfloat16),
            pltpu.VMEM((PEERS, TILE, rank), jnp.float32),
            pltpu.VMEM((n_col, rank), jnp.float32),
            pltpu.VMEM((PEERS, TILE, rank), jnp.bfloat16),
            pltpu.SemaphoreType.DMA((PEERS,)),
            pltpu.SemaphoreType.DMA((1,)),
            pltpu.SemaphoreType.DMA((n_slot // GROUP,)),
            pltpu.SemaphoreType.DMA((1,)),
            pltpu.SemaphoreType.DMA((PEERS + n_col // TILE,)),
        ],
        compiler_params=pltpu.CompilerParams(vmem_limit_bytes=47 * 1024 * 1024),
        cost_estimate=pl.CostEstimate(
            flops=6 * n_slot * TILE * TILE * rank, bytes_accessed=9 << 20, transcendentals=0
        ),
        name="stratum_%d" % stratum,
    )(*smem_args, tiles, noise, *rows, *panels)
    return out[:n_part], out[n_part]


def copy_kernel(source, target, buffer, sem):
    load = pltpu.make_async_copy(source, buffer, sem.at[0])
    load.start()
    load.wait()
    store = pltpu.make_async_copy(buffer, target, sem.at[1])
    store.start()
    store.wait()


def copied(value):
    free = pl.BlockSpec(memory_space=pl.ANY)
    return pl.pallas_call(
        copy_kernel,
        out_shape=jax.ShapeDtypeStruct(value.shape, value.dtype),
        in_specs=[free],
        out_specs=free,
        scratch_shapes=[pltpu.VMEM(value.shape, value.dtype), pltpu.SemaphoreType.DMA((2,))],
        name="copied",
    )(value)


def finish_kernel(step, matching, *refs):
    part_in, (shard, noise, v_in, v_other) = refs[:5], refs[5:9]
    row_out, col_out, part_s, own_s, v_s, sem = refs[9:]
    stratum = noise.shape[0] - 1
    panel_in = pltpu.make_async_copy(v_in, v_s, sem.at[7])
    other_in = pltpu.make_async_copy(v_other, v_s, sem.at[7])
    panel_out = pltpu.make_async_copy(v_s, col_out, sem.at[8])
    loads = [
        pltpu.make_async_copy(part_in[i].at[pl.ds(0, TILE)], part_s.at[i], sem.at[i])
        for i in range(5)
    ]
    loads.append(pltpu.make_async_copy(shard, own_s.at[0], sem.at[5]))
    loads.append(pltpu.make_async_copy(noise.at[stratum], own_s.at[1], sem.at[6]))
    crosses = matching[stratum, 0] & 1
    pl.when(crosses == 0)(panel_in.start)
    pl.when(crosses == 1)(other_in.start)
    for copy in loads:
        copy.start()
    panel_in.wait()
    panel_out.start()
    for copy in loads:
        copy.wait()
    total = wide(part_s[0]) + wide(part_s[1]) + wide(part_s[2]) + wide(part_s[3]) + wide(part_s[4])
    h = step[stratum]
    root = jnp.sqrt(jnp.full((1, 1), h, jnp.float32))
    current = wide(own_s[0])
    moved = current + (0.5 * h) * (total - prior_precision * current) + root * wide(own_s[1])
    row_out[...] = moved.astype(jnp.bfloat16)
    panel_out.wait()


def finish(step_sizes, matching, terms, shard, row_noise, panel, other):
    free = pl.BlockSpec(memory_space=pl.ANY)
    return pl.pallas_call(
        finish_kernel,
        out_shape=[jax.ShapeDtypeStruct(x.shape, jnp.bfloat16) for x in (shard, panel)],
        in_specs=[pl.BlockSpec(memory_space=pltpu.SMEM)] * 2 + [free] * 9,
        out_specs=[pl.BlockSpec(memory_space=pltpu.VMEM), free],
        scratch_shapes=[
            pltpu.VMEM((5,) + shard.shape, jnp.bfloat16),
            pltpu.VMEM((2,) + shard.shape, jnp.bfloat16),
            pltpu.VMEM(panel.shape, jnp.bfloat16),
            pltpu.SemaphoreType.DMA((9,)),
        ],
        compiler_params=pltpu.CompilerParams(vmem_limit_bytes=16 * 1024 * 1024),
        name="finish",
    )(step_sizes, matching, *terms, shard, row_noise, panel, other)


def on_device(
    row_factor,
    col_factor,
    tiles,
    tile_rows,
    tile_cols,
    tile_counts,
    matching,
    row_noise,
    col_noise,
    step_sizes,
):
    me = jnp.stack([lax.axis_index("cols"), is_inner(lax.axis_index("rows"))]).astype(jnp.int32)
    blocks = lax.axis_size("rows")
    first = matching[0, 0]

    def move(mask, panel):
        return swap(panel, "rows", mask) if mask else copied(panel)

    def route(flip, panel):
        return lax.switch(
            first >> 1, [functools.partial(move, k ^ flip) for k in range(0, blocks, 2)], panel
        )

    def kernel(stratum, rows, *panels):
        smem_args = (me, step_sizes, tile_rows, tile_cols, tile_counts)
        return stratum_step(stratum, smem_args, tiles, col_noise, rows, panels)

    def gather_rows(shard):
        partner = swap(shard, "cols", 4)
        near = swap_near(shard, 0)
        far = [swap(after(partner, near[k - 1]), "cols", k) for k in (1, 2, 3)]
        return [shard] + near + [partner] + far

    def scatter_rows(parts, far, panel):
        far_sum = wide(parts[4]) + wide(far[0]) + wide(far[1]) + wide(far[2])
        far_sum = far_sum.astype(jnp.bfloat16)
        partner = swap(far_sum, "cols", 4)
        near = swap_near([after(part, far_sum) for part in parts[:4]], 0)
        partner, panel = lax.optimization_barrier((partner, panel))
        return [parts[0]] + near + [partner], panel

    rows = gather_rows(row_factor)
    panel = jnp.where(first & 1 == 1, swap(col_factor, "rows", 1), col_factor)
    panel = route(0, after(panel, *rows[1:5]))
    parts, panel = kernel(0, rows, panel)

    terms, inner = scatter_rows(parts, swap_near(parts, 4), swap_mirror(panel, 1))
    total = wide(terms[0]) + wide(terms[1]) + wide(terms[2]) + wide(terms[3]) + wide(terms[4])
    shard = langevin(row_factor, total, row_noise[0], step_sizes[0]).astype(jnp.bfloat16)
    rows = gather_rows(shard)
    outer = swap_mirror(after(panel, *rows[1:5]), 0)
    parts, panel = kernel(1, rows, inner, outer)

    terms = [parts[0]] + swap_near(parts, 0)
    panel = route(blocks - 2, panel)
    far_sum = sum(wide(term[TILE:]) for term in terms)
    far_sum = after(far_sum.astype(jnp.bfloat16), panel)
    partner = swap(far_sum, "cols", 4)
    other = swap(after(panel, far_sum), "rows", 1)
    return finish(step_sizes, matching, terms + [partner], shard, row_noise, panel, other)


def solution(mesh):
    return jax.shard_map(
        on_device,
        mesh=mesh,
        in_specs=(
            P(("rows", "cols"), None),
            P(("rows", "cols"), None),
            P(None, "rows", "cols", None, None, None),
            P(None, "rows", "cols", None),
            P(None, "rows", "cols", None),
            P(None, "rows", "cols"),
            P(),
            P(None, ("rows", "cols"), None),
            P(None, ("rows", "cols"), None),
            P(),
        ),
        out_specs=(P(("rows", "cols"), None), P(("rows", "cols"), None)),
        check_vma=False,
    )
```

```python
import functools

import jax
import jax.numpy as jnp
from jax import lax
from jax.experimental import pallas as pl
from jax.experimental.pallas import tpu as pltpu
from jax.sharding import PartitionSpec as P

TILE = 256
PEERS = 8
GROUP = 4

prior_precision = 1.0


def swap(value, axis, mask):
    return lax.ppermute(value, axis, [(i, i ^ mask) for i in range(lax.axis_size(axis))])


def is_inner(row):
    return (row >> 1 ^ row >> 2) & 1


def swap_mirror(value, inner):
    size = lax.axis_size("rows")
    pairs = [(i, i ^ size - 1) for i in range(size) if is_inner(i) == inner]
    return lax.ppermute(value, "rows", pairs)


def langevin(current, gradient, gaussian, step_size):
    current_wide = current.astype(jnp.float32)
    return (
        current_wide
        + 0.5 * step_size * (gradient - prior_precision * current_wide)
        + jnp.sqrt(step_size) * gaussian.astype(jnp.float32)
    )


def wide(value):
    return value.astype(jnp.float32)


def after(value, *others):
    return lax.optimization_barrier((value,) + others)[0]


def swap_near(parts, base):
    pick = (lambda k: parts[base + k]) if isinstance(parts, (list, tuple)) else (lambda k: parts)
    return [swap(pick(k), "cols", k) for k in (1, 2, 3)]


def stratum_kernel(stratum, n_in, me, step, row_pick, col_pick, count, tiles, noise, *refs):
    u_in, refs = refs[:PEERS], refs[PEERS:]
    v_in, refs = refs[:n_in], refs[n_in:]
    n_part = PEERS if n_in == 1 else PEERS // 2
    q_out, v_out, refs = refs[:n_part], refs[n_part], refs[n_part + 1 :]
    u_s, v_s, t_s, n_s, r_acc, c_acc, q_s, u_sem, v_sem, t_sem, n_sem, o_sem = refs
    n_group = t_s.shape[0] // GROUP
    loads = [pltpu.make_async_copy(u_in[k], u_s.at[k], u_sem.at[k]) for k in range(PEERS)]
    panel_loads = [pltpu.make_async_copy(panel, v_s, v_sem.at[0]) for panel in v_in]

    def tile_load(i):
        span = pl.ds(i * GROUP, GROUP)
        return pltpu.make_async_copy(tiles.at[stratum, 0, 0, span], t_s.at[span], t_sem.at[i])

    noise_load = pltpu.make_async_copy(noise.at[stratum], n_s, n_sem.at[0])
    if n_in == 1:
        panel_loads[0].start()
    else:
        for inner, copy in zip((1, 0), panel_loads):
            pl.when(me[1] == inner)(copy.start)
    for copy in loads:
        copy.start()
    for i in range(n_group):
        tile_load(i).start()
    noise_load.start()
    r_acc[...] = jnp.zeros_like(r_acc)
    c_acc[...] = jnp.zeros_like(c_acc)
    for copy in loads + panel_loads[:1]:
        copy.wait()
    total = count[stratum, 0, 0]

    def group(i, carry):
        tile_load(i).wait()
        work = []
        for j in range(GROUP):
            t = i * GROUP + j
            r = row_pick[stratum, 0, 0, t] ^ me[0]
            c = pl.ds(pl.multiple_of(col_pick[stratum, 0, 0, t] * TILE, TILE), TILE)
            predicted = lax.dot_general(
                u_s[r], v_s[c], (((1,), (1,)), ((), ())), preferred_element_type=jnp.float32
            )
            residual = (wide(t_s[t]) - predicted).astype(jnp.bfloat16)
            work.append((r, c, jnp.where(t < total, residual, jnp.zeros_like(residual))))
        for r, c, residual in work:
            r_acc[r] += jnp.dot(residual, v_s[c], preferred_element_type=jnp.float32)
            c_acc[c] += lax.dot_general(
                residual, u_s[r], (((0,), (0,)), ((), ())), preferred_element_type=jnp.float32
            )
        return carry

    def unused(i, carry):
        tile_load(i).wait()
        return carry

    used = (total + GROUP - 1) // GROUP
    lax.fori_loop(0, used, group, 0)
    lax.fori_loop(used, n_group, unused, 0)
    stores = []
    for k in (5, 6, 7, 4, 1, 2, 3, 0):
        q_s[k] = r_acc[k].astype(jnp.bfloat16)
        if n_in == 1:
            target = q_out[k]
        else:
            target = q_out[k % 4].at[pl.ds(k // 4 * TILE, TILE)]
        stores.append(pltpu.make_async_copy(q_s.at[k], target, o_sem.at[k]))
        stores[-1].start()
    h = step[stratum]
    root = jnp.sqrt(jnp.full((1, 1), h, jnp.float32))
    noise_load.wait()
    for low in range(0, v_s.shape[0], TILE):
        rows = pl.ds(low, TILE)
        current = wide(v_s[rows])
        moved = current + (0.5 * h) * (c_acc[rows] - prior_precision * current) + root * wide(n_s[rows])
        v_s[rows] = moved.astype(jnp.bfloat16)
        stores.append(pltpu.make_async_copy(v_s.at[rows], v_out.at[rows], o_sem.at[len(stores)]))
        stores[-1].start()
    for copy in stores:
        copy.wait()


def stratum_step(stratum, smem_args, tiles, noise, rows, panels):
    n_col, rank = noise.shape[1:]
    n_slot = tiles.shape[3]
    smem = pl.BlockSpec(memory_space=pltpu.SMEM)
    free = pl.BlockSpec(memory_space=pl.ANY)
    n_part = PEERS if len(panels) == 1 else PEERS // 2
    part = jax.ShapeDtypeStruct((PEERS // n_part * TILE, rank), jnp.bfloat16)
    out = pl.pallas_call(
        functools.partial(stratum_kernel, stratum, len(panels)),
        out_shape=[part] * n_part + [jax.ShapeDtypeStruct((n_col, rank), jnp.bfloat16)],
        in_specs=[smem] * 5 + [free] * (2 + PEERS + len(panels)),
        out_specs=[free] * (n_part + 1),
        scratch_shapes=[
            pltpu.VMEM((PEERS, TILE, rank), jnp.bfloat16),
            pltpu.VMEM((n_col, rank), jnp.bfloat16),
            pltpu.VMEM((n_slot, TILE, TILE), jnp.bfloat16),
            pltpu.VMEM((n_col, rank), jnp.bfloat16),
            pltpu.VMEM((PEERS, TILE, rank), jnp.float32),
            pltpu.VMEM((n_col, rank), jnp.float32),
            pltpu.VMEM((PEERS, TILE, rank), jnp.bfloat16),
            pltpu.SemaphoreType.DMA((PEERS,)),
            pltpu.SemaphoreType.DMA((1,)),
            pltpu.SemaphoreType.DMA((n_slot // GROUP,)),
            pltpu.SemaphoreType.DMA((1,)),
            pltpu.SemaphoreType.DMA((PEERS + n_col // TILE,)),
        ],
        compiler_params=pltpu.CompilerParams(vmem_limit_bytes=47 * 1024 * 1024),
        cost_estimate=pl.CostEstimate(
            flops=6 * n_slot * TILE * TILE * rank, bytes_accessed=9 << 20, transcendentals=0
        ),
        name="stratum_%d" % stratum,
    )(*smem_args, tiles, noise, *rows, *panels)
    return out[:n_part], out[n_part]


def copy_kernel(source, target, buffer, sem):
    load = pltpu.make_async_copy(source, buffer, sem.at[0])
    load.start()
    load.wait()
    store = pltpu.make_async_copy(buffer, target, sem.at[1])
    store.start()
    store.wait()


def copied(value):
    free = pl.BlockSpec(memory_space=pl.ANY)
    return pl.pallas_call(
        copy_kernel,
        out_shape=jax.ShapeDtypeStruct(value.shape, value.dtype),
        in_specs=[free],
        out_specs=free,
        scratch_shapes=[pltpu.VMEM(value.shape, value.dtype), pltpu.SemaphoreType.DMA((2,))],
        name="copied",
    )(value)


def finish_kernel(step, matching, *refs):
    part_in, (shard, noise, v_in, v_other) = refs[:5], refs[5:9]
    row_out, col_out, part_s, own_s, v_s, sem = refs[9:]
    stratum = noise.shape[0] - 1
    panel_in = pltpu.make_async_copy(v_in, v_s, sem.at[7])
    other_in = pltpu.make_async_copy(v_other, v_s, sem.at[7])
    panel_out = pltpu.make_async_copy(v_s, col_out, sem.at[8])
    loads = [
        pltpu.make_async_copy(part_in[i].at[pl.ds(0, TILE)], part_s.at[i], sem.at[i])
        for i in range(5)
    ]
    loads.append(pltpu.make_async_copy(shard, own_s.at[0], sem.at[5]))
    loads.append(pltpu.make_async_copy(noise.at[stratum], own_s.at[1], sem.at[6]))
    crosses = matching[stratum, 0] & 1
    pl.when(crosses == 0)(panel_in.start)
    pl.when(crosses == 1)(other_in.start)
    for copy in loads:
        copy.start()
    panel_in.wait()
    panel_out.start()
    for copy in loads:
        copy.wait()
    total = wide(part_s[0]) + wide(part_s[1]) + wide(part_s[2]) + wide(part_s[3]) + wide(part_s[4])
    h = step[stratum]
    root = jnp.sqrt(jnp.full((1, 1), h, jnp.float32))
    current = wide(own_s[0])
    moved = current + (0.5 * h) * (total - prior_precision * current) + root * wide(own_s[1])
    row_out[...] = moved.astype(jnp.bfloat16)
    panel_out.wait()


def finish(step_sizes, matching, terms, shard, row_noise, panel, other):
    free = pl.BlockSpec(memory_space=pl.ANY)
    return pl.pallas_call(
        finish_kernel,
        out_shape=[jax.ShapeDtypeStruct(x.shape, jnp.bfloat16) for x in (shard, panel)],
        in_specs=[pl.BlockSpec(memory_space=pltpu.SMEM)] * 2 + [free] * 9,
        out_specs=[pl.BlockSpec(memory_space=pltpu.VMEM), free],
        scratch_shapes=[
            pltpu.VMEM((5,) + shard.shape, jnp.bfloat16),
            pltpu.VMEM((2,) + shard.shape, jnp.bfloat16),
            pltpu.VMEM(panel.shape, jnp.bfloat16),
            pltpu.SemaphoreType.DMA((9,)),
        ],
        compiler_params=pltpu.CompilerParams(vmem_limit_bytes=16 * 1024 * 1024),
        name="finish",
    )(step_sizes, matching, *terms, shard, row_noise, panel, other)


def on_device(
    row_factor,
    col_factor,
    tiles,
    tile_rows,
    tile_cols,
    tile_counts,
    matching,
    row_noise,
    col_noise,
    step_sizes,
):
    me = jnp.stack([lax.axis_index("cols"), is_inner(lax.axis_index("rows"))]).astype(jnp.int32)
    blocks = lax.axis_size("rows")
    first = matching[0, 0]

    def move(mask, panel):
        return swap(panel, "rows", mask) if mask else copied(panel)

    def route(flip, panel):
        return lax.switch(
            first >> 1, [functools.partial(move, k ^ flip) for k in range(0, blocks, 2)], panel
        )

    def kernel(stratum, rows, *panels):
        smem_args = (me, step_sizes, tile_rows, tile_cols, tile_counts)
        return stratum_step(stratum, smem_args, tiles, col_noise, rows, panels)

    def gather_rows(shard, panel=None):
        partner = swap(shard, "cols", 4)
        near = swap_near(shard, 0)
        if panel is not None:
            partner, panel, *near = lax.optimization_barrier((partner, panel, *near))
        far = [swap(after(partner, near[k - 1]), "cols", k) for k in (1, 2, 3)]
        return [shard] + near + [partner] + far, panel

    def scatter_rows(parts, far, panel):
        far_sum = wide(parts[4]) + wide(far[0]) + wide(far[1]) + wide(far[2])
        far_sum = far_sum.astype(jnp.bfloat16)
        partner = swap(far_sum, "cols", 4)
        near = swap_near([after(part, far_sum) for part in parts[:4]], 0)
        partner, panel = lax.optimization_barrier((partner, panel))
        return [parts[0]] + near + [partner], panel

    panel = jnp.where(first & 1 == 1, swap(col_factor, "rows", 1), col_factor)
    rows, panel = gather_rows(row_factor, panel)
    panel = route(0, after(panel, *rows[1:5]))
    parts, panel = kernel(0, rows, panel)

    terms, inner = scatter_rows(parts, swap_near(parts, 4), swap_mirror(panel, 1))
    total = wide(terms[0]) + wide(terms[1]) + wide(terms[2]) + wide(terms[3]) + wide(terms[4])
    shard = langevin(row_factor, total, row_noise[0], step_sizes[0]).astype(jnp.bfloat16)
    rows, _ = gather_rows(shard)
    outer = swap_mirror(after(panel, *rows[1:5]), 0)
    parts, panel = kernel(1, rows, inner, outer)

    terms = [parts[0]] + swap_near(parts, 0)
    panel = route(blocks - 2, panel)
    far_sum = sum(wide(term[TILE:]) for term in terms)
    far_sum = after(far_sum.astype(jnp.bfloat16), panel)
    partner = swap(far_sum, "cols", 4)
    other = swap(after(panel, far_sum), "rows", 1)
    return finish(step_sizes, matching, terms + [partner], shard, row_noise, panel, other)


def solution(mesh):
    return jax.shard_map(
        on_device,
        mesh=mesh,
        in_specs=(
            P(("rows", "cols"), None),
            P(("rows", "cols"), None),
            P(None, "rows", "cols", None, None, None),
            P(None, "rows", "cols", None),
            P(None, "rows", "cols", None),
            P(None, "rows", "cols"),
            P(),
            P(None, ("rows", "cols"), None),
            P(None, ("rows", "cols"), None),
            P(),
        ),
        out_specs=(P(("rows", "cols"), None), P(("rows", "cols"), None)),
        check_vma=False,
    )
```
